512 devices in a mesh: row: 16 (over z, y_lo), col: 32 (over x, y_hi, core).
Axes of the slice: x: 4, y: 8 (y_hi: 4, y_lo: 2; y = y_hi * 2 + y_lo), z: 8, core: 2. Of those that a mesh axis runs over, the one named last changes fastest.
Arguments:
- ratings: bfloat16 [16, 96, 512, 512], P('row', 'col'), may hold values from 0 to 3, as said below
- tile_items: int32 [16, 96], P('row', 'col'), may hold values from 0 to 3, as said below
- tile_live: int32 [16, 96], P('row', 'col'), may hold values from 0 to 1, as said below
- item_factors: float32 [65536, 256], P(('col', 'row'))
Outputs:
- user_factors: float32 [8192, 256], P(('row', 'col'))
The draws below stay inside these ranges and needn't reach their ends.
Inputs may be any that keep to these rules, and one draw needn't show every extreme that they name: `tile_items`: on each device the 3 slots name distinct item blocks. `tile_live`: the first slot of each device (every third entry of the second dimension, starting at 0) is live. `ratings`: entries are zero or positive.
All inputs are finite; a program needn't handle non-finite values.
Results may differ from the reference program's by a relative error of at most 0.0003.
Values sent between devices are 32-bit elements; how exact they have to be, the bound alone decides.
A program may use at most 64 MiB of HBM per device.

```python
import math
import jax
import jax.numpy as jnp
from jax import lax

K = 256
TB = 512
ITEM_BLK = 4
TILES_DEV = 3
ITERS = 3
ITEMS = 65536
N_ROW = 16
N_COL = 32


def draw_ratings(key, part):
    key = jax.random.fold_in(key, 11)

    def one_row(row_index):
        row_key = jax.random.fold_in(key, row_index)
        first_key, second_key = jax.random.split(row_key)
        shape = (N_COL * TILES_DEV, TB, TB)
        present = jax.random.randint(first_key, shape, 0, 3) == 0
        values = jnp.exp(jax.random.uniform(second_key, shape, jnp.float32, math.log(0.1), math.log(3.0)))
        return jnp.where(present, values, 0.0).astype(jnp.bfloat16)
    return lax.map(one_row, jnp.arange(N_ROW, dtype=jnp.int32))


def draw_tile_items(key, part):
    key = jax.random.fold_in(key, 12)
    scores = jax.random.randint(key, (N_ROW, N_COL, ITEM_BLK), 0, 1 << 20) * ITEM_BLK + jnp.arange(ITEM_BLK, dtype=jnp.int32)
    chosen = jnp.argsort(scores, axis=-1, stable=True)[:, :, :TILES_DEV]
    return chosen.reshape(N_ROW, N_COL * TILES_DEV).astype(jnp.int32)


def draw_tile_live(key, part):
    key = jax.random.fold_in(key, 13)
    flags = jax.random.randint(key, (N_ROW, N_COL, TILES_DEV), 0, 2)
    first_slot = jnp.arange(TILES_DEV, dtype=jnp.int32) == 0
    flags = jnp.where(first_slot, 1, flags)
    return flags.reshape(N_ROW, N_COL * TILES_DEV).astype(jnp.int32)


def draw_item_factors(key, part):
    key = jax.random.fold_in(key, 14)
    keys = jax.random.split(key, 3)
    column_scale = jnp.exp(jax.random.uniform(keys[0], (1, K), jnp.float32, 0.0, math.log(10.0)))
    rising = 1.0 + 2.0 * jnp.arange(ITEMS, dtype=jnp.float32)[:, None] / ITEMS
    row_scale = jnp.exp(jax.random.uniform(keys[1], (ITEMS, 1), jnp.float32, 0.0, math.log(3.0))) * rising
    base_values = jax.random.normal(keys[2], (ITEMS, K), jnp.float32)
    return (0.003 * base_values * column_scale * row_scale).astype(jnp.float32)


def setup_inputs(seed: int = 0) -> dict:
    splits = jax.random.split(jax.random.key(seed), 5)
    ratings = draw_ratings(jax.random.fold_in(splits[4], 71), 0)
    tile_items = draw_tile_items(jax.random.fold_in(splits[4], 71), 0)
    tile_live = draw_tile_live(jax.random.fold_in(splits[4], 71), 0)
    item_factors = draw_item_factors(jax.random.fold_in(splits[4], 71), 0)
    return {"ratings": ratings, "tile_items": tile_items, "tile_live": tile_live, "item_factors": item_factors}


CONFIDENCE_SCALE = 40.0
RIDGE = 1.0
DIVISOR_GUARD = 1e-20
HIGH = lax.Precision.HIGHEST


def rated_weights(tile_block, live_flag, preference):
    rating = tile_block.astype(jnp.float32)
    if preference:
        weight = jnp.where(rating > 0.0, 1.0 + CONFIDENCE_SCALE * rating, 0.0)
    else:
        weight = CONFIDENCE_SCALE * rating
    return weight * live_flag.astype(jnp.float32)


def tile_term(tile_block, live_flag, item_rows, vectors):
    if vectors is None:
        inner_part = rated_weights(tile_block, live_flag, True)
    else:
        scores = lax.dot_general(vectors, item_rows, (((1,), (1,)), ((), ())), precision=HIGH, preferred_element_type=jnp.float32)
        inner_part = rated_weights(tile_block, live_flag, False) * scores
    return jnp.dot(inner_part, item_rows, precision=HIGH, preferred_element_type=jnp.float32)


def reference(ratings, tile_items, tile_live, item_factors):
    gram_matrix = lax.dot_general(item_factors, item_factors, (((0,), (0,)), ((), ())), precision=HIGH, preferred_element_type=jnp.float32)
    slot_count = N_COL * TILES_DEV

    def partial_sums(vectors):
        row_terms = []
        for row_index in range(N_ROW):
            own_rows = None if vectors is None else vectors[row_index * TB:(row_index + 1) * TB]

            def advance(running, slot_index):
                tile_block = ratings[row_index, slot_index]
                live_flag = tile_live[row_index, slot_index]
                offset = ((slot_index // TILES_DEV) * ITEM_BLK + tile_items[row_index, slot_index]) * TB
                item_rows = lax.dynamic_slice_in_dim(item_factors, offset.astype(jnp.int32), TB, 0)
                return running + tile_term(tile_block, live_flag, item_rows, own_rows), None

            running, _ = lax.scan(advance, jnp.zeros((TB, K), jnp.float32), jnp.arange(slot_count, dtype=jnp.int32))
            row_terms.append(running)
        return jnp.concatenate(row_terms, axis=0)

    rhs = partial_sums(None)
    solution = jnp.zeros_like(rhs)
    residual = rhs
    direction = rhs
    norm_now = jnp.sum(residual * residual, axis=1, keepdims=True)
    for iteration in range(ITERS):
        product_rows = jnp.dot(direction, gram_matrix, precision=HIGH, preferred_element_type=jnp.float32) + RIDGE * direction + partial_sums(direction)
        curvature = jnp.sum(direction * product_rows, axis=1, keepdims=True)
        step_size = norm_now / (curvature + DIVISOR_GUARD)
        solution = solution + step_size * direction
        residual = residual - step_size * product_rows
        norm_next = jnp.sum(residual * residual, axis=1, keepdims=True)
        direction = residual + (norm_next / (norm_now + DIVISOR_GUARD)) * direction
        norm_now = norm_next
    return solution
```

```python
import functools

import jax
import jax.numpy as jnp
from jax import lax
from jax.experimental import pallas as pl
from jax.experimental.pallas import tpu as pltpu
from jax.sharding import PartitionSpec as P

ITERS = 3
CONFIDENCE_SCALE = 40.0
RIDGE = 1.0
DIVISOR_GUARD = 1e-20

K = 256
TB = 512
BLOCKS = 4
SLOTS = 3
Z = 8
CHIPS = 16
STREAMS = 1
OWN = 16 // STREAMS
HALF = CHIPS * OWN
CUT = 56
SHARE = 128
MESH = pl.DeviceIdType.MESH
F32 = jnp.float32
BF16 = jnp.bfloat16

NN = (((1,), (0,)), ((), ()))
NT = (((1,), (1,)), ((), ()))
TN = (((0,), (0,)), ((), ()))


def split(value):
    high = value.astype(BF16)
    return high, (value - high.astype(F32)).astype(BF16)


def dot(a, b, dims):
    return lax.dot_general(a, b, dims, preferred_element_type=F32)


def dot3(a, b, dims):
    return dot(a[0], b[0], dims) + (dot(a[1], b[0], dims) + dot(a[0], b[1], dims))


def kernel(
    tile_ref, live_ref, ratings_ref, items_ref, out_ref,
    items, raw, weights, item_high, item_low, scaled_high, scaled_low, gram_high, gram_low,
    vectors, partial, from_core, summed, from_chips, direction, lane_sums, lane_core, lane_total, lane_chips,
    load_sem, z_send, z_recv, y_send, y_recv, core_send, core_recv, reduce_send, reduce_recv,
    gather_send, gather_recv, back_send, back_recv, last_send, last_recv,
):
    row = lax.axis_index("row")
    col = lax.axis_index("col")
    z, y_lo = row // 2, row % 2
    chip, core = col // 2, col % 2
    other_core = 1 - core

    def chip_at(offset):
        return ((chip // 4 + offset // 4) % 4) * 4 + (chip % 4 + offset % 4) % 4

    def opposite(offset):
        return (-(offset // 4) % 4) * 4 + -(offset % 4) % 4

    to_core = (row, chip * 2 + other_core)
    to_y = (z * 2 + 1 - y_lo, col)
    to_z = {1: (((z + 1) % Z) * 2 + y_lo, col), -1: (((z + Z - 1) % Z) * 2 + y_lo, col)}
    to_chip = {k: (row, chip_at(k) * 2 + core) for k in range(1, CHIPS)}

    pending = []

    def send(src, dst, send_sem, recv_sem, device):
        copy = pltpu.make_async_remote_copy(
            src_ref=src, dst_ref=dst, send_sem=send_sem, recv_sem=recv_sem, device_id=device, device_id_type=MESH
        )
        copy.start()
        pending.append(copy)

    def arrived(dst, send_sem, recv_sem, device):
        pltpu.make_async_remote_copy(
            src_ref=dst, dst_ref=dst, send_sem=send_sem, recv_sem=recv_sem, device_id=device, device_id_type=MESH
        ).wait_recv()

    def item_rows(z_of, y_of, first, count):
        return items.at[pl.ds(pl.multiple_of((z_of * 2 + y_of) * SHARE + first, 8), count)]

    own_load = pltpu.make_async_copy(items_ref, item_rows(z, y_lo, 0, SHARE), load_sem.at[0])
    own_load.start()
    rating_loads = [
        pltpu.make_async_copy(ratings_ref.at[:, :, c], raw.at[:, c], load_sem.at[1 + c]) for c in range(2)
    ]
    for load in rating_loads:
        load.start()

    barrier = pltpu.get_barrier_semaphore()
    neighbours = [to_core, to_y, to_z[1], to_z[-1]] + list(to_chip.values())
    for device in neighbours:
        pl.semaphore_signal(barrier, inc=1, device_id=device, device_id_type=MESH)
    own_load.wait()
    pl.semaphore_wait(barrier, len(neighbours))

    def z_piece(kind, z_of):
        if kind == 0:
            return item_rows(z_of, y_lo, 0, CUT)
        if kind == 1:
            return item_rows(z_of, y_lo, CUT, SHARE - CUT)
        return item_rows(z_of, 1 - y_lo, 0, CUT)

    reach = {(0, 1): 4, (0, -1): 3, (1, 1): 3, (1, -1): 4, (2, 1): 4, (2, -1): 3}

    def z_index(kind, way, hop):
        return (kind * 2 + (way + 1) // 2) * 4 + hop - 1

    def z_source(way, hop):
        return (z + Z - way * hop) % Z

    def z_send_piece(kind, way, hop):
        piece = z_piece(kind, z_source(way, hop - 1))
        index = z_index(kind, way, hop)
        send(piece, piece, z_send.at[index], z_recv.at[index], to_z[way])

    def y_send_piece(index, z_of, first, count):
        piece = item_rows(z_of, y_lo, first, count)
        send(piece, piece, y_send.at[index], y_recv.at[index], to_y)

    y_send_piece(0, z, 0, CUT)
    for kind in (0, 1):
        for way in (1, -1):
            z_send_piece(kind, way, 1)
    y_send_piece(1, z, CUT, SHARE - CUT)
    arrived(item_rows(z, 1 - y_lo, 0, CUT), y_send.at[0], y_recv.at[0], to_y)
    for way in (1, -1):
        z_send_piece(2, way, 1)
    crossing = [(1, z)]
    for hop in range(1, 5):
        for kind in (0, 1, 2):
            for way in (1, -1):
                if hop > reach[kind, way]:
                    continue
                source = z_source(way, hop)
                index = z_index(kind, way, hop)
                arrived(z_piece(kind, source), z_send.at[index], z_recv.at[index], to_z[-way])
                if hop < reach[kind, way]:
                    z_send_piece(kind, way, hop + 1)
                if kind == 1:
                    y_index = len(crossing) + 1
                    y_send_piece(y_index, source, CUT, SHARE - CUT)
                    crossing.append((y_index, source))
    for load in rating_loads:
        load.wait()
    for slot in range(SLOTS):
        for half in range(2):
            block = raw[slot, half].astype(F32)
            for stream in range(STREAMS):
                part = block[:, stream * OWN:(stream + 1) * OWN, :]
                weights[stream, slot, half * HALF:(half + 1) * HALF, :] = part.reshape(HALF, TB)
    for y_index, source in crossing:
        piece = item_rows(source, 1 - y_lo, CUT, SHARE - CUT)
        arrived(piece, y_send.at[y_index], y_recv.at[y_index], to_y)

    live = [live_ref[0, slot].astype(F32) for slot in range(SLOTS)]
    gram_even = jnp.zeros((K, K), F32)
    gram_odd = jnp.zeros((K, K), F32)
    for block in range(BLOCKS):
        high, low = split(items[block * TB:(block + 1) * TB, :])
        gram_even += dot(high, high, TN)
        gram_odd += dot(high, low, TN)
    gram_high[...], gram_low[...] = split(gram_even + (gram_odd + gram_odd.T))
    for slot in range(SLOTS):
        block = jnp.zeros((TB, K), F32)
        for index in range(BLOCKS):
            block += (tile_ref[0, slot] == index).astype(F32) * items[index * TB:(index + 1) * TB, :]
        item_high[slot], item_low[slot] = split(block)
        scaled_high[slot], scaled_low[slot] = split(block * (CONFIDENCE_SCALE * live[slot]))

    def reduce_start(phase, stream):
        send(
            partial.at[phase, stream, other_core], from_core.at[phase, stream],
            core_send.at[phase, stream], core_recv.at[phase, stream], to_core,
        )

    def reduce_middle(phase, stream):
        arrived(from_core.at[phase, stream], core_send.at[phase, stream], core_recv.at[phase, stream], to_core)
        summed[phase, stream] = partial[phase, stream, core] + from_core[phase, stream]
        for k in range(1, CHIPS):
            start = pl.multiple_of(chip_at(k) * OWN, OWN)
            send(
                summed.at[phase, stream, pl.ds(start, OWN)], from_chips.at[phase, stream, k],
                reduce_send.at[phase, stream, k], reduce_recv.at[phase, stream, k], to_chip[k],
            )

    def reduce_finish(phase, stream):
        total = summed[phase, stream, pl.ds(pl.multiple_of(chip * OWN, OWN), OWN), :]
        for k in range(1, CHIPS):
            arrived(
                from_chips.at[phase, stream, k], reduce_send.at[phase, stream, k],
                reduce_recv.at[phase, stream, k], to_chip[k],
            )
            total += from_chips[phase, stream, k]
        return total

    def gather_start(phase, stream, value):
        mine = pl.ds(pl.multiple_of(chip * OWN, OWN), OWN)
        vectors[phase, stream, core, mine, :] = value
        piece = vectors.at[phase, stream, core, mine]
        for k in range(1, CHIPS):
            send(piece, piece, gather_send.at[phase, stream, k], gather_recv.at[phase, stream, k], to_chip[k])

    def gather_middle(phase, stream):
        for k in range(1, CHIPS):
            start = pl.multiple_of(chip_at(opposite(k)) * OWN, OWN)
            piece = vectors.at[phase, stream, core, pl.ds(start, OWN)]
            arrived(piece, gather_send.at[phase, stream, k], gather_recv.at[phase, stream, k], to_chip[k])
        half = vectors.at[phase, stream, core]
        send(half, half, back_send.at[phase, stream], back_recv.at[phase, stream], to_core)

    def gather_finish(phase, stream):
        half = vectors.at[phase, stream, other_core]
        arrived(half, back_send.at[phase, stream], back_recv.at[phase, stream], to_core)

    def half_rows(half):
        return pl.ds(pl.multiple_of(half * HALF, HALF), HALF)

    for stream in range(STREAMS):
        for half in (other_core, core):
            total = jnp.zeros((HALF, K), F32)
            for slot in range(SLOTS):
                rating = weights[stream, slot, half_rows(half), :]
                weight = jnp.where(rating > 0.0, 1.0 + CONFIDENCE_SCALE * rating, 0.0) * live[slot]
                total += dot3(split(weight), (item_high[slot], item_low[slot]), NN)
            partial[0, stream, half] = total
        reduce_start(0, stream)
    for stream in range(STREAMS):
        reduce_middle(0, stream)
    state = []
    for stream in range(STREAMS):
        rhs = reduce_finish(0, stream)
        gather_start(0, stream, rhs)
        norm = jnp.sum(rhs * rhs, axis=1, keepdims=True)
        state.append((jnp.zeros_like(rhs), rhs, rhs, norm))

    for phase in range(1, ITERS):
        for stream in range(STREAMS):
            gather_middle(phase - 1, stream)
            for order in range(2):
                half = core if order == 0 else other_core
                if order == 1:
                    gather_finish(phase - 1, stream)
                vector = split(vectors[phase - 1, stream, half])
                total = dot3(vector, (gram_high[...], gram_low[...]), NN)
                for slot in range(SLOTS):
                    scores = dot3(vector, (item_high[slot], item_low[slot]), NT)
                    inner = split(weights[stream, slot, half_rows(half), :] * scores)
                    total += dot3(inner, (scaled_high[slot], scaled_low[slot]), NN)
                partial[phase, stream, half] = total
            reduce_start(phase, stream)
        for stream in range(STREAMS):
            reduce_middle(phase, stream)
        for stream in range(STREAMS):
            found, residual, along, norm = state[stream]
            image = reduce_finish(phase, stream) + RIDGE * along
            curvature = jnp.sum(along * image, axis=1, keepdims=True)
            step = norm / (curvature + DIVISOR_GUARD)
            found = found + step * along
            residual = residual - step * image
            norm_next = jnp.sum(residual * residual, axis=1, keepdims=True)
            along = residual + norm_next / (norm + DIVISOR_GUARD) * along
            gather_start(phase, stream, along)
            state[stream] = (found, residual, along, norm_next)

    phase = ITERS - 1
    lane_sums[...] = jnp.zeros_like(lane_sums)
    ones = jnp.ones((8, 128), F32)
    for stream in range(STREAMS):
        gather_middle(phase, stream)
        for order in range(2):
            half = core if order == 0 else other_core
            if order == 1:
                gather_finish(phase, stream)
            rows = vectors[phase, stream, half]
            vector = split(rows)
            squares = rows * dot3(vector, (gram_high[...], gram_low[...]), NN)
            squares = squares[:, :128] + squares[:, 128:]
            for slot in range(SLOTS):
                scores = dot3(vector, (item_high[slot], item_low[slot]), NT)
                weighted = weights[stream, slot, half_rows(half), :] * (scores * scores)
                folded = (weighted[:, :128] + weighted[:, 128:256]) + (weighted[:, 256:384] + weighted[:, 384:])
                squares += (CONFIDENCE_SCALE * live[slot]) * folded
            packed = lax.dot_general(
                ones, squares, NT, precision=lax.Precision.HIGHEST, preferred_element_type=F32
            )
            for piece in range(HALF // 128):
                lane_sums[half, stream, piece, :] = packed[0, piece * 128:(piece + 1) * 128]
    send(lane_sums, lane_core, last_send.at[0], last_recv.at[0], to_core)
    arrived(lane_core, last_send.at[0], last_recv.at[0], to_core)
    lane_total[...] = lane_sums[...] + lane_core[...]
    for k in range(1, CHIPS):
        send(lane_total, lane_chips.at[k], last_send.at[k], last_recv.at[k], to_chip[k])
    total = lane_total[...]
    for k in range(1, CHIPS):
        arrived(lane_chips.at[k], last_send.at[k], last_recv.at[k], to_chip[k])
        total += lane_chips[k]
    owners = 128 // OWN
    for stream in range(STREAMS):
        found, residual, along, norm = state[stream]
        pick = jnp.zeros((8, 128), F32)
        for half in range(2):
            for piece in range(HALF // 128):
                mine = jnp.logical_and(core == half, chip // owners == piece)
                pick = jnp.where(mine, jnp.broadcast_to(total[half, stream, piece][None, :], (8, 128)), pick)
        lanes = lax.broadcasted_iota(jnp.int32, (OWN, 128), 1)
        users = lax.broadcasted_iota(jnp.int32, (OWN, 128), 0)
        pick = jnp.broadcast_to(pick[:1], (OWN, 128))
        curvature = jnp.sum(jnp.where(lanes == (chip % owners) * OWN + users, pick, 0.0), axis=1, keepdims=True)
        curvature = curvature + RIDGE * jnp.sum(along * along, axis=1, keepdims=True)
        out_ref[stream * OWN:(stream + 1) * OWN, :] = found + norm / (curvature + DIVISOR_GUARD) * along

    for copy in pending:
        copy.wait_send()


def per_device(ratings, tile_items, tile_live, item_factors):
    by_owner = ratings.reshape(SLOTS, CHIPS, 2, 16, TB)
    dma = pltpu.SemaphoreType.DMA
    anywhere = pl.BlockSpec(memory_space=pl.ANY)
    scalar = pl.BlockSpec(memory_space=pltpu.SMEM)
    vmem = pltpu.VMEM
    return pl.pallas_call(
        kernel,
        out_shape=jax.ShapeDtypeStruct((16, K), F32),
        in_specs=[scalar, scalar, anywhere, anywhere],
        out_specs=pl.BlockSpec(memory_space=vmem),
        scratch_shapes=[
            vmem((BLOCKS * TB, K), F32),
            vmem((SLOTS, 2, CHIPS, 16, TB), BF16),
            vmem((STREAMS, SLOTS, 2 * HALF, TB), F32),
            vmem((SLOTS, TB, K), BF16),
            vmem((SLOTS, TB, K), BF16),
            vmem((SLOTS, TB, K), BF16),
            vmem((SLOTS, TB, K), BF16),
            vmem((K, K), BF16),
            vmem((K, K), BF16),
            vmem((ITERS, STREAMS, 2, HALF, K), F32),
            vmem((ITERS, STREAMS, 2, HALF, K), F32),
            vmem((ITERS, STREAMS, HALF, K), F32),
            vmem((ITERS, STREAMS, HALF, K), F32),
            vmem((ITERS, STREAMS, CHIPS, OWN, K), F32),
            vmem((STREAMS, OWN, K), F32),
            vmem((2, STREAMS, 8, 128), F32),
            vmem((2, STREAMS, 8, 128), F32),
            vmem((2, STREAMS, 8, 128), F32),
            vmem((CHIPS, 2, STREAMS, 8, 128), F32),
            dma((3,)),
            dma((24,)), dma((24,)),
            dma((10,)), dma((10,)),
            dma((ITERS, STREAMS)), dma((ITERS, STREAMS)),
            dma((ITERS, STREAMS, CHIPS)), dma((ITERS, STREAMS, CHIPS)),
            dma((ITERS, STREAMS, CHIPS)), dma((ITERS, STREAMS, CHIPS)),
            dma((ITERS, STREAMS)), dma((ITERS, STREAMS)),
            dma((CHIPS,)), dma((CHIPS,)),
        ],
        compiler_params=pltpu.CompilerParams(
            collective_id=0, has_side_effects=True, vmem_limit_bytes=48 << 20
        ),
        cost_estimate=pl.CostEstimate(flops=14_000_000_000, bytes_accessed=4_000_000, transcendentals=0),
        name="half_step",
    )(tile_items, tile_live, by_owner, item_factors)


def solution(mesh):
    placed = (
        P("row", "col", None, None),
        P("row", "col"),
        P("row", "col"),
        P(("col", "row"), None),
    )
    return jax.shard_map(
        per_device, mesh=mesh, in_specs=placed, out_specs=P(("row", "col"), None), check_vma=False
    )
```

```python
import functools

import jax
import jax.numpy as jnp
from jax import lax
from jax.experimental import pallas as pl
from jax.experimental.pallas import tpu as pltpu
from jax.sharding import PartitionSpec as P

ITERS = 3
CONFIDENCE_SCALE = 40.0
RIDGE = 1.0
DIVISOR_GUARD = 1e-20

K = 256
TB = 512
BLOCKS = 4
SLOTS = 3
Z = 8
CHIPS = 16
STREAMS = 2
OWN = 16 // STREAMS
HALF = CHIPS * OWN
ROWS = 2 * HALF
CUT = 56
SHARE = 128
MESH = pl.DeviceIdType.MESH
F32 = jnp.float32
BF16 = jnp.bfloat16

NN = (((1,), (0,)), ((), ()))
NT = (((1,), (1,)), ((), ()))
TN = (((0,), (0,)), ((), ()))


def split(value):
    high = value.astype(BF16)
    return high, (value - high.astype(F32)).astype(BF16)


def dot(a, b, dims):
    return lax.dot_general(a, b, dims, preferred_element_type=F32)


def dot3(a, b, dims):
    return dot(a[0], b[0], dims) + (dot(a[1], b[0], dims) + dot(a[0], b[1], dims))


def kernel(
    tile_hbm, live_hbm, ratings_ref, items_ref, out_ref,
    tile_ref, live_ref, items, raw, weights, item_high, item_low, scaled_high, scaled_low, gram_high, gram_low,
    gram_even, gram_odd, right,
    vectors, partial, from_core, summed, from_chips, direction, lane_sums, lane_core, lane_total, lane_chips,
    load_sem, z_send, z_recv, y_send, y_recv, core_send, core_recv, reduce_send, reduce_recv,
    gather_send, gather_recv, back_send, back_recv, last_send, last_recv,
):
    row = lax.axis_index("row")
    col = lax.axis_index("col")
    z, y_lo = lax.div(row, 2), lax.rem(row, 2)
    chip, core = lax.div(col, 2), lax.rem(col, 2)
    chip_x, chip_y = lax.div(chip, 4), lax.rem(chip, 4)
    other_core = 1 - core

    ring_x = [chip_x] + [lax.rem(chip_x + step, 4) for step in range(1, 4)]
    ring_y = [chip_y] + [lax.rem(chip_y + step, 4) for step in range(1, 4)]
    chip_at = [ring_x[k // 4] * 4 + ring_y[k % 4] for k in range(CHIPS)]
    owner_rows = [pl.ds(pl.multiple_of(chip_at[k] * OWN, OWN), OWN) for k in range(CHIPS)]
    ring_z = [z] + [lax.rem(z + step, Z) for step in range(1, Z)]

    def opposite(offset):
        return (-(offset // 4) % 4) * 4 + -(offset % 4) % 4

    to_core = (row, chip * 2 + other_core)
    to_y = (z * 2 + 1 - y_lo, col)
    to_z = {1: (ring_z[1] * 2 + y_lo, col), -1: (ring_z[Z - 1] * 2 + y_lo, col)}
    offsets = sorted(
        range(1, CHIPS), key=lambda k: min(k // 4, 4 - k // 4) + 2 * min(k % 4, 4 - k % 4), reverse=True
    )
    to_chip = {k: (row, chip_at[k] * 2 + core) for k in range(1, CHIPS)}

    pending = []

    def send(src, dst, send_sem, recv_sem, device):
        copy = pltpu.make_async_remote_copy(
            src_ref=src, dst_ref=dst, send_sem=send_sem, recv_sem=recv_sem, device_id=device, device_id_type=MESH
        )
        copy.start()
        pending.append(copy)

    def arrived(dst, send_sem, recv_sem, device):
        pltpu.make_async_remote_copy(
            src_ref=dst, dst_ref=dst, send_sem=send_sem, recv_sem=recv_sem, device_id=device, device_id_type=MESH
        ).wait_recv()

    share_start = {
        (step, side): (ring_z[step] * 2 + (1 - y_lo if side else y_lo)) * SHARE for step in range(Z) for side in (0, 1)
    }

    def item_rows(step, side, first, count):
        return items.at[pl.ds(pl.multiple_of(share_start[step, side] + first, 8), count)]

    own_load = pltpu.make_async_copy(items_ref, item_rows(0, 0, 0, SHARE), load_sem.at[0])
    own_load.start()
    rating_loads = [
        pltpu.make_async_copy(ratings_ref.at[:, :, c], raw.at[:, c], load_sem.at[1 + c]) for c in range(2)
    ]
    scalar_loads = [
        pltpu.make_async_copy(tile_hbm, tile_ref, load_sem.at[3]),
        pltpu.make_async_copy(live_hbm, live_ref, load_sem.at[4]),
    ]
    for load in scalar_loads + rating_loads:
        load.start()

    barrier = pltpu.get_barrier_semaphore()
    neighbours = [to_core, to_y, to_z[1], to_z[-1]] + list(to_chip.values())
    for device in neighbours:
        pl.semaphore_signal(barrier, inc=1, device_id=device, device_id_type=MESH)
    own_load.wait()
    pl.semaphore_wait(barrier, len(neighbours))

    def chunk_tasks(step):
        z_of = ring_z[step]
        block_of = lax.div(z_of, 2)
        chunk = pl.ds(pl.multiple_of(z_of * (2 * SHARE), 2 * SHARE), 2 * SHARE)
        columns = pl.ds(pl.multiple_of(lax.rem(z_of, 2) * (2 * SHARE), 2 * SHARE), 2 * SHARE)

        def gram_terms():
            high, low = split(items[chunk, :])
            gram_even[...] += dot(high, high, TN)
            gram_odd[...] += dot(high, low, TN)

        def right_terms(stream, first):
            users = pl.ds(first, 256)
            scales = [
                (tile_ref[0, slot] == block_of).astype(F32) * live_ref[0, slot].astype(F32) for slot in range(SLOTS)
            ]
            rating = weights[stream, 0, users, columns] * scales[0]
            for slot in range(1, SLOTS):
                rating += weights[stream, slot, users, columns] * scales[slot]
            weight = jnp.where(rating > 0.0, 1.0 + CONFIDENCE_SCALE * rating, 0.0)
            right[stream, users, :] += dot3(split(weight), split(items[chunk, :]), NN)

        tasks.append(gram_terms)
        for stream in range(STREAMS):
            for first in range(0, ROWS, 256):
                tasks.append(functools.partial(right_terms, stream, first))

    tasks = []

    pieces = [(1, CUT, 40), (1, CUT + 40, SHARE - CUT - 40)]
    pieces += [(0, 0, 32), (0, 32, CUT - 32), (2, 0, 32), (2, 32, CUT - 32)]
    reach = {(0, 1): 4, (0, -1): 3, (1, 1): 3, (1, -1): 4, (2, 1): 4, (2, -1): 3}

    def z_source(way, hop):
        return -way * hop % Z

    def z_piece(number, way, hop):
        kind, first, count = pieces[number]
        return item_rows(z_source(way, hop), kind // 2, first, count)

    def z_index(number, way, hop):
        return (number * 2 + (way + 1) // 2) * 4 + hop - 1

    crossings = {}
    crossing_count = []

    def cross(key, step, first, count):
        index = len(crossing_count)
        crossing_count.append(index)
        crossings.setdefault(key, []).append((index, step, first, count))
        piece = item_rows(step, 0, first, count)
        send(piece, piece, y_send.at[index], y_recv.at[index], to_y)

    def crossed(key):
        for index, step, first, count in crossings.pop(key):
            arrived(item_rows(step, 1, first, count), y_send.at[index], y_recv.at[index], to_y)

    for kind, first, count in pieces:
        if kind == 0:
            cross(("first", first), 0, first, count)
    for hop in range(1, 6):
        for number, (kind, first, count) in enumerate(pieces):
            for way in (1, -1):
                index = z_index(number, way, hop - 1)
                if 1 < hop <= reach[kind, way] + 1:
                    arrived(z_piece(number, way, hop - 1), z_send.at[index], z_recv.at[index], to_z[-way])
                elif hop == 1 and kind == 2 and way == 1:
                    crossed(("first", first))
                if hop <= reach[kind, way]:
                    piece = z_piece(number, way, hop - 1)
                    index = z_index(number, way, hop)
                    send(piece, piece, z_send.at[index], z_recv.at[index], to_z[way])
                if kind == 1 and (way == 1 if hop == 1 else hop <= reach[kind, way] + 1):
                    cross(("rest", hop - 1, way), z_source(way, hop - 1), first, count)
                if tasks and hop > 2:
                    tasks.pop(0)()
        if hop == 1:
            for load in scalar_loads + rating_loads:
                load.wait()
            for slot in range(SLOTS):
                for half in range(2):
                    block = raw[slot, half].astype(F32)
                    for stream in range(STREAMS):
                        part = block[:, stream * OWN:(stream + 1) * OWN, :]
                        weights[stream, slot, half * HALF:(half + 1) * HALF, :] = part.reshape(HALF, TB)
            gram_even[...] = jnp.zeros_like(gram_even)
            gram_odd[...] = jnp.zeros_like(gram_odd)
            right[...] = jnp.zeros_like(right)
        elif hop == 2:
            crossed(("rest", 0, 1))
            chunk_tasks(0)
        else:
            for way in (1, -1):
                crossed(("rest", hop - 2, way))
                chunk_tasks(z_source(way, hop - 2))
    while tasks:
        tasks.pop(0)()
    crossed(("rest", 4, -1))
    chunk_tasks(z_source(1, 4))
    while tasks:
        tasks.pop(0)()

    live = [live_ref[0, slot].astype(F32) for slot in range(SLOTS)]

    def pick_items(slot):
        block = jnp.zeros((TB, K), F32)
        for index in range(BLOCKS):
            block += (tile_ref[0, slot] == index).astype(F32) * items[index * TB:(index + 1) * TB, :]
        item_high[slot], item_low[slot] = split(block)
        scaled_high[slot], scaled_low[slot] = split(block * (CONFIDENCE_SCALE * live[slot]))

    def reduce_start(phase, stream):
        send(
            partial.at[phase, stream, other_core], from_core.at[phase, stream],
            core_send.at[phase, stream], core_recv.at[phase, stream], to_core,
        )

    def reduce_middle(phase, stream):
        arrived(from_core.at[phase, stream], core_send.at[phase, stream], core_recv.at[phase, stream], to_core)
        summed[phase, stream] = partial[phase, stream, core] + from_core[phase, stream]
        for k in offsets:
            send(
                summed.at[phase, stream, owner_rows[k]], from_chips.at[phase, stream, k],
                reduce_send.at[phase, stream, k], reduce_recv.at[phase, stream, k], to_chip[k],
            )

    def reduce_finish(phase, stream):
        total = summed[phase, stream, owner_rows[0], :]
        for k in range(1, CHIPS):
            arrived(
                from_chips.at[phase, stream, k], reduce_send.at[phase, stream, k],
                reduce_recv.at[phase, stream, k], to_chip[k],
            )
            total += from_chips[phase, stream, k]
        return total

    def gather_start(phase, stream, value):
        mine = owner_rows[0]
        vectors[phase, stream, core, mine, :] = value
        piece = vectors.at[phase, stream, core, mine]
        for k in offsets:
            send(piece, piece, gather_send.at[phase, stream, k], gather_recv.at[phase, stream, k], to_chip[k])

    def gather_middle(phase, stream):
        for k in range(1, CHIPS):
            piece = vectors.at[phase, stream, core, owner_rows[opposite(k)]]
            arrived(piece, gather_send.at[phase, stream, k], gather_recv.at[phase, stream, k], to_chip[k])
        half = vectors.at[phase, stream, core]
        send(half, half, back_send.at[phase, stream], back_recv.at[phase, stream], to_core)

    def gather_finish(phase, stream):
        half = vectors.at[phase, stream, other_core]
        arrived(half, back_send.at[phase, stream], back_recv.at[phase, stream], to_core)

    for stream in range(STREAMS):
        partial[0, stream] = right[stream].reshape(2, HALF, K)
        reduce_start(0, stream)
    pick_items(0)
    for stream in range(STREAMS):
        reduce_middle(0, stream)
    for slot in range(1, SLOTS):
        pick_items(slot)
    gram_high[...], gram_low[...] = split(gram_even[...] + (gram_odd[...] + gram_odd[...].T))
    state = []
    for stream in range(STREAMS):
        rhs = reduce_finish(0, stream)
        gather_start(0, stream, rhs)
        norm = jnp.sum(rhs * rhs, axis=1, keepdims=True)
        state.append((jnp.zeros_like(rhs), rhs, rhs, norm))

    for phase in range(1, ITERS):
        for stream in range(STREAMS):
            gather_middle(phase - 1, stream)
            if stream:
                reduce_middle(phase, stream - 1)
            gather_finish(phase - 1, stream)
            vector = split(vectors[phase - 1, stream].reshape(ROWS, K))
            total = dot3(vector, (gram_high[...], gram_low[...]), NN)
            for slot in range(SLOTS):
                scores = dot3(vector, (item_high[slot], item_low[slot]), NT)
                inner = split(weights[stream, slot] * scores)
                total += dot3(inner, (scaled_high[slot], scaled_low[slot]), NN)
            partial[phase, stream] = total.reshape(2, HALF, K)
            reduce_start(phase, stream)
        reduce_middle(phase, STREAMS - 1)
        for stream in range(STREAMS):
            found, residual, along, norm = state[stream]
            image = reduce_finish(phase, stream) + RIDGE * along
            curvature = jnp.sum(along * image, axis=1, keepdims=True)
            step = norm / (curvature + DIVISOR_GUARD)
            found = found + step * along
            residual = residual - step * image
            norm_next = jnp.sum(residual * residual, axis=1, keepdims=True)
            along = residual + norm_next / (norm + DIVISOR_GUARD) * along
            gather_start(phase, stream, along)
            state[stream] = (found, residual, along, norm_next)

    phase = ITERS - 1
    lane_sums[...] = jnp.zeros_like(lane_sums)
    ones = jnp.ones((8, 128), F32)

    def lane_row(half, stream, piece):
        return (half * STREAMS + stream) * (HALF // 128) + piece

    for stream in range(STREAMS):
        gather_middle(phase, stream)
        gather_finish(phase, stream)
        rows = vectors[phase, stream].reshape(ROWS, K)
        vector = split(rows)
        squares = rows * dot3(vector, (gram_high[...], gram_low[...]), NN)
        squares = squares[:, :128] + squares[:, 128:]
        for slot in range(SLOTS):
            scores = dot3(vector, (item_high[slot], item_low[slot]), NT)
            weighted = weights[stream, slot] * (scores * scores)
            folded = (weighted[:, :128] + weighted[:, 128:256]) + (weighted[:, 256:384] + weighted[:, 384:])
            squares += (CONFIDENCE_SCALE * live[slot]) * folded
        packed = lax.dot_general(
            ones, squares, NT, precision=lax.Precision.HIGHEST, preferred_element_type=F32
        )
        for half in range(2):
            for piece in range(HALF // 128):
                start = half * HALF + piece * 128
                lane_sums[lane_row(half, stream, piece), :] = packed[0, start:start + 128]
    send(lane_sums, lane_core, last_send.at[0], last_recv.at[0], to_core)
    arrived(lane_core, last_send.at[0], last_recv.at[0], to_core)
    lane_total[...] = lane_sums[...] + lane_core[...]
    for k in offsets:
        send(lane_total, lane_chips.at[k], last_send.at[k], last_recv.at[k], to_chip[k])
    total = lane_total[...]
    for k in range(1, CHIPS):
        arrived(lane_chips.at[k], last_send.at[k], last_recv.at[k], to_chip[k])
        total += lane_chips[k]
    owners = 128 // OWN
    for stream in range(STREAMS):
        found, residual, along, norm = state[stream]
        pick = jnp.zeros((8, 128), F32)
        for half in range(2):
            for piece in range(HALF // 128):
                mine = jnp.logical_and(core == half, lax.div(chip, owners) == piece)
                pick = jnp.where(mine, jnp.broadcast_to(total[lane_row(half, stream, piece)][None, :], (8, 128)), pick)
        lanes = lax.broadcasted_iota(jnp.int32, (OWN, 128), 1)
        users = lax.broadcasted_iota(jnp.int32, (OWN, 128), 0)
        pick = jnp.broadcast_to(pick[:1], (OWN, 128))
        curvature = jnp.sum(jnp.where(lanes == lax.rem(chip, owners) * OWN + users, pick, 0.0), axis=1, keepdims=True)
        curvature = curvature + RIDGE * jnp.sum(along * along, axis=1, keepdims=True)
        out_ref[stream * OWN:(stream + 1) * OWN, :] = found + norm / (curvature + DIVISOR_GUARD) * along

    for copy in pending:
        copy.wait_send()


def per_device(ratings, tile_items, tile_live, item_factors):
    by_owner = ratings.reshape(SLOTS, CHIPS, 2, 16, TB)
    dma = pltpu.SemaphoreType.DMA
    in_hbm = pl.BlockSpec(memory_space=pltpu.HBM)
    vmem = pltpu.VMEM
    return pl.pallas_call(
        kernel,
        out_shape=jax.ShapeDtypeStruct((16, K), F32),
        in_specs=[in_hbm] * 4,
        out_specs=pl.BlockSpec(memory_space=vmem),
        scratch_shapes=[
            pltpu.SMEM((1, SLOTS), jnp.int32),
            pltpu.SMEM((1, SLOTS), jnp.int32),
            vmem((BLOCKS * TB, K), F32),
            vmem((SLOTS, 2, CHIPS, 16, TB), BF16),
            vmem((STREAMS, SLOTS, ROWS, TB), F32),
            vmem((SLOTS, TB, K), BF16),
            vmem((SLOTS, TB, K), BF16),
            vmem((SLOTS, TB, K), BF16),
            vmem((SLOTS, TB, K), BF16),
            vmem((K, K), BF16),
            vmem((K, K), BF16),
            vmem((K, K), F32),
            vmem((K, K), F32),
            vmem((STREAMS, ROWS, K), F32),
            vmem((ITERS, STREAMS, 2, HALF, K), F32),
            vmem((ITERS, STREAMS, 2, HALF, K), F32),
            vmem((ITERS, STREAMS, HALF, K), F32),
            vmem((ITERS, STREAMS, HALF, K), F32),
            vmem((ITERS, STREAMS, CHIPS, OWN, K), F32),
            vmem((STREAMS, OWN, K), F32),
            vmem((8, 128), F32),
            vmem((8, 128), F32),
            vmem((8, 128), F32),
            vmem((CHIPS, 8, 128), F32),
            dma((5,)),
            dma((48,)), dma((48,)),
            dma((18,)), dma((18,)),
            dma((ITERS, STREAMS)), dma((ITERS, STREAMS)),
            dma((ITERS, STREAMS, CHIPS)), dma((ITERS, STREAMS, CHIPS)),
            dma((ITERS, STREAMS, CHIPS)), dma((ITERS, STREAMS, CHIPS)),
            dma((ITERS, STREAMS)), dma((ITERS, STREAMS)),
            dma((CHIPS,)), dma((CHIPS,)),
        ],
        compiler_params=pltpu.CompilerParams(
            collective_id=0, has_side_effects=True, vmem_limit_bytes=63 << 20
        ),
        cost_estimate=pl.CostEstimate(flops=14_000_000_000, bytes_accessed=4_000_000, transcendentals=0),
        name="half_step",
    )(tile_items, tile_live, by_owner, item_factors)


def solution(mesh):
    placed = (
        P("row", "col", None, None),
        P("row", "col"),
        P("row", "col"),
        P(("col", "row"), None),
    )
    return jax.shard_map(
        per_device, mesh=mesh, in_specs=placed, out_specs=P(("row", "col"), None), check_vma=False
    )
```
